32 devices in a mesh: pool: 4 (over z), tp: 8 (over y, x, core).
Axes of the slice: x: 2, y: 2, z: 4, core: 2. Of those that a mesh axis runs over, the one named last changes fastest.
Arguments:
- tokens: bfloat16 [512, 8192], P(('pool', 'tp')), may hold values from -4 to 4
- lengths: int32 [4, 4], P('pool'), may hold values from 1 to 64, 128 in all within a row
- hit_pages: int32 [4, 4, 4], P('pool'), may hold values from 0 to 2047, as said below
- new_owner: int32 [4, 4], P('pool'), may hold values from 0 to 3, as said below
- w_query: bfloat16 [8192, 8192], P('pool', 'tp'), may hold values from -0.125 to 0.125
- w_keyval: bfloat16 [4096, 4096], P('pool', 'tp'), may hold values from -0.0625 to 0.0625
- w_out: bfloat16 [8192, 8192], P('tp', 'pool'), may hold values from -0.0625 to 0.0625
- pool_pages: bfloat16 [2048, 8, 8192], P('pool', 'tp'), may hold values from -65 to 65
Outputs:
- mixed: float32 [512, 8192], P(('pool', 'tp'))
- new_store: bfloat16 [32, 8, 8192], P('pool', 'tp')
The draws below stay inside these ranges and needn't reach their ends.
Inputs may be any that keep to these rules, and one draw needn't show every extreme that they name: Page p of the pool lies on pool index p // 512. In every group g at most 6 of the 16 entries of hit_pages[g] lie on one pool index, and some pool index holds exactly 6 of them in every group. A page may appear more than once. `new_owner`: in every group at most 2 of its 4 pages go to one pool index, and some pool index receives exactly 2 from every group. Row g holds the lengths of the 4 requests packed in group g, in order, and sums to 128.
All inputs are finite; a program needn't handle non-finite values.
Results may differ from the reference program's by a relative error of at most 0.009.
Values may be sent and summed in bfloat16 or wider, within the bound.
A program may use at most 128 MiB of HBM per device.

```python
import math
import jax
import jax.numpy as jnp
import numpy as np
from jax import lax

D = 8192
H = 64
KVH = 8
HD = 128
PAGE = 32
REQS = 4
HITS = 4
PAGES_DEV = 512
CAPF = 6
CAPN = 2
GROUP = 128
TOKENS = 512
NEWP = 4
NHIT = 16
POOL_PAGES = 2048
KV_PART = 256
N_POOL = 4
N_TP = 8


def spread_owners(base_key, groups, count_items, owners, capacity):
    hot_owner = jax.random.randint(jax.random.fold_in(base_key, 1), (), 0, owners)
    seat_owner = jnp.arange((owners - 1) * capacity, dtype=jnp.int32) // capacity
    seat_owner = seat_owner + (seat_owner >= hot_owner).astype(jnp.int32)
    group_keys = jax.random.split(jax.random.fold_in(base_key, 2), groups)

    def one_group(group_key):
        chosen = jax.random.permutation(group_key, seat_owner)[:count_items - capacity]
        listed = jnp.concatenate([jnp.full((capacity,), hot_owner, jnp.int32), chosen])
        return jax.random.permutation(jax.random.fold_in(group_key, 3), listed)
    return jax.vmap(one_group)(group_keys)


def draw_hit_pages(key, part):
    base_key = jax.random.fold_in(key, 11)
    owners = spread_owners(base_key, N_POOL, REQS * HITS, N_POOL, CAPF)
    within = jax.random.randint(jax.random.fold_in(base_key, 5), (N_POOL, REQS * HITS), 0, PAGES_DEV)
    return (owners * PAGES_DEV + within).astype(jnp.int32).reshape(N_POOL, REQS, HITS)


def draw_new_owner(key, part):
    base_key = jax.random.fold_in(key, 23)
    return spread_owners(base_key, N_POOL, NEWP, N_POOL, CAPN).astype(jnp.int32)


def draw_pool_pages(key, part):
    base_key = jax.random.fold_in(key, 37)
    dims = (N_POOL * PAGES_DEV, PAGE, 2 * KVH * HD)
    first_key = jax.random.fold_in(base_key, 1)
    values = jnp.clip(jax.random.normal(first_key, dims, jnp.float32), -4.0, 4.0)
    values = values.reshape(dims[0], PAGE, N_TP, KV_PART).transpose(0, 2, 1, 3).reshape(dims[0], N_TP, PAGE * KV_PART)
    return values.astype(jnp.bfloat16)


def steps_of(stream_key, shape, cuts, least, high):
    loudness, own = 1.0, jax.random.fold_in(stream_key, 6)
    for dim, blocks in cuts:
        steps = jnp.exp(jax.random.uniform(jax.random.fold_in(own, dim), (blocks,), jnp.float32, least / len(cuts), high / len(cuts)))
        loudness = loudness * jnp.repeat(steps, shape[dim] // blocks).reshape([-1 if axis == dim else 1 for axis in range(len(shape))])
    return loudness


def length_profile(amount, total, most, slope):
    portions = [(1 << 20) // math.isqrt(standing ** slope) + 1 for standing in range(2, amount + 1)]
    rest, holding = total - most - (amount - 1), [1] * (amount - 1)
    while rest > 0:
        candidates = [i for i in range(amount - 1) if holding[i] < most]
        whole, budget = sum([portions[i] for i in candidates]), rest
        for i in candidates:
            extra = min(most - holding[i], max(1, budget * portions[i] // whole), rest)
            holding[i] = holding[i] + extra
            rest = rest - extra
    return np.array([most] + holding)


def uneven_parts(own_key, number_of, total, bound, lean):
    if number_of == 2:
        one = jax.random.randint(own_key, (), max(1, total - bound), min(bound, total - 1) + 1)
        return jnp.stack([one, total - one])
    tallies = jnp.asarray(length_profile(number_of, total, bound, lean), jnp.int32)
    couples = (number_of - 1) // 2
    source_of, receiver = tallies[1:1 + 2 * couples:2], tallies[2:2 + 2 * couples:2]
    slack = jnp.minimum(source_of - 1, bound - receiver)
    passed = jax.random.randint(jax.random.fold_in(own_key, 1), (couples,), 0, 1 << 20) % (slack + 1)
    tallies = tallies.at[1:1 + 2 * couples:2].set(source_of - passed).at[2:2 + 2 * couples:2].set(receiver + passed)
    return tallies[jax.random.permutation(jax.random.fold_in(own_key, 2), number_of)]


def bell_draw(key, extent, spread, reach, cuts=(), held_as=jnp.bfloat16):
    level = steps_of(key, extent, cuts, -0.22, 0.18) if cuts else 1.0
    result = jax.random.normal(key, extent, jnp.float32) * spread * level
    return jnp.minimum(jnp.maximum(result, -reach), reach).astype(held_as)


def setup_inputs(seed: int = 0) -> dict:
    splits = jax.random.split(jax.random.key(seed), 9)
    tokens = bell_draw(splits[0], (TOKENS, D), 0.5, 4.0, ((0, 32),))
    lengths = jax.vmap(lambda own: uneven_parts(own, REQS, GROUP, GROUP // 2, 2))(jax.random.split(splits[1], N_POOL)).reshape((N_POOL, REQS)).astype(jnp.int32)
    hit_pages = draw_hit_pages(jax.random.fold_in(splits[8], 71), 0)
    new_owner = draw_new_owner(jax.random.fold_in(splits[8], 71), 0)
    w_query = bell_draw(splits[4], (D, H * HD), (D // 4) ** -0.5, 0.125, ((0, 4), (1, 8)))
    w_keyval = bell_draw(splits[5], (D // 2, 2 * 2 * KVH * HD), D ** -0.5, 0.0625, ((0, 4), (1, 8)))
    w_out = bell_draw(splits[6], (H * HD, D), (H * HD) ** -0.5, 0.0625, ((0, 8), (1, 4)))
    pool_pages = draw_pool_pages(jax.random.fold_in(splits[8], 71), 0)
    return {"tokens": tokens, "lengths": lengths, "hit_pages": hit_pages, "new_owner": new_owner, "w_query": w_query, "w_keyval": w_keyval, "w_out": w_out, "pool_pages": pool_pages}


EPSILON = 1e-06
ROPE_BASE = 1000000.0

def rotate(values, positions):
    half = values.shape[-1] // 2
    steps_range = jnp.arange(half, dtype=jnp.float32)
    frequency = ROPE_BASE ** (-2.0 * steps_range / values.shape[-1])
    angles = positions.astype(jnp.float32)[:, None, None] * frequency[None, None, :]
    cosine = jnp.cos(angles)
    sine = jnp.sin(angles)
    first_half = values[..., :half]
    second_half = values[..., half:]
    return jnp.concatenate([first_half * cosine - second_half * sine, second_half * cosine + first_half * sine], axis=-1)

def request_layout(lengths_row):
    ends_at = jnp.cumsum(lengths_row).astype(jnp.int32)
    starts_at = (ends_at - lengths_row).astype(jnp.int32)
    token_index = jnp.arange(GROUP, dtype=jnp.int32)
    request_ids = lax.optimization_barrier(jnp.sum((token_index[:, None] >= ends_at[None, :]).astype(jnp.int32), axis=1)).astype(jnp.int32)
    chosen = request_ids[:, None] == jnp.arange(REQS, dtype=jnp.int32)[None, :]
    start_of = lax.optimization_barrier(jnp.sum(jnp.where(chosen, starts_at[None, :], 0), axis=1)).astype(jnp.int32)
    positions = token_index - start_of + HITS * PAGE
    return (token_index, request_ids, positions)

def slot_table(owners_row, capacity, seats):
    count_items = owners_row.shape[0]
    item_index = jnp.arange(count_items, dtype=jnp.int32)
    earlier_same = (owners_row[:, None] == owners_row[None, :]) & (item_index[None, :] < item_index[:, None])
    slots = lax.optimization_barrier(jnp.sum(earlier_same.astype(jnp.int32), axis=1)).astype(jnp.int32)
    targets = owners_row.astype(jnp.int32) * capacity + slots
    seat_index = jnp.arange(seats, dtype=jnp.int32)
    return targets[:, None] == seat_index[None, :]

def one_group(tokens_group, lengths_row, hits_row, owners_row, w_query, w_keyval, w_out, pool_pages):
    tokens_wide = tokens_group.astype(jnp.float32)
    normed = (tokens_wide * lax.rsqrt(lax.optimization_barrier(jnp.mean(tokens_wide * tokens_wide, axis=1, keepdims=True)) + EPSILON)).astype(jnp.bfloat16)
    token_index, request_ids, positions = request_layout(lengths_row)
    queries = jnp.dot(normed, w_query, preferred_element_type=jnp.float32).reshape(GROUP, H, HD)
    queries = rotate(queries, positions).astype(jnp.bfloat16)
    keyval = jnp.dot(normed, w_keyval, preferred_element_type=jnp.float32).astype(jnp.bfloat16).reshape(GROUP, KVH, 2 * HD)
    new_keys = rotate(keyval[:, :, :HD].astype(jnp.float32), positions).astype(jnp.bfloat16)
    new_kv = jnp.concatenate([new_keys, keyval[:, :, HD:]], axis=2)
    cached = jnp.take(pool_pages, hits_row.reshape(-1).astype(jnp.int32), axis=0).reshape(NHIT * PAGE, KVH, 2 * HD)
    all_kv = jnp.concatenate([cached, new_kv], axis=0).astype(jnp.float32)
    key_request = jnp.concatenate([jnp.arange(NHIT * PAGE, dtype=jnp.int32) // (HITS * PAGE), request_ids])
    key_order = jnp.concatenate([jnp.full((NHIT * PAGE,), -1, jnp.int32), token_index])
    visible = (request_ids[:, None] == key_request[None, :]) & (key_order[None, :] <= token_index[:, None])
    grouped = queries.astype(jnp.float32).reshape(GROUP, KVH, H // KVH, HD)
    scores = jnp.einsum('gjmd,kjd->jmgk', grouped, all_kv[:, :, :HD]) / math.sqrt(HD)
    scores = jnp.where(visible[None, None], scores, -jnp.inf)
    weights = lax.optimization_barrier(jax.nn.softmax(scores, axis=-1).astype(jnp.bfloat16)).astype(jnp.float32)
    attended = jnp.einsum('jmgk,kjd->gjmd', weights, all_kv[:, :, HD:]).reshape(GROUP, H * HD).astype(jnp.bfloat16)
    head_width = H * HD // N_TP
    head_pieces = attended.reshape(GROUP, N_TP, head_width).transpose(1, 0, 2)
    out_rows = w_out.reshape(N_TP, head_width, D)

    def add_part(running, weights_pair):
        term = jnp.dot(weights_pair[0], weights_pair[1], preferred_element_type=jnp.float32)
        term = lax.optimization_barrier(term.astype(jnp.bfloat16)).astype(jnp.float32)
        return (running + term, None)
    summed, _ignored = lax.scan(add_part, jnp.zeros((GROUP, D), jnp.float32), (head_pieces, out_rows))
    mixed = tokens_wide + summed
    new_pages = new_kv.reshape(NEWP, PAGE * KVH * 2 * HD)
    placed = slot_table(owners_row, CAPN, N_POOL * CAPN).astype(jnp.bfloat16)
    outgoing = jnp.dot(placed.T, new_pages, preferred_element_type=jnp.float32).astype(jnp.bfloat16)
    outgoing = outgoing.reshape(N_POOL, CAPN, PAGE, N_TP, KV_PART).transpose(0, 1, 3, 2, 4)
    return (mixed, outgoing.reshape(N_POOL, CAPN, N_TP, PAGE * KV_PART))

def reference(tokens, lengths, hit_pages, new_owner, w_query, w_keyval, w_out, pool_pages):
    keyval_matrix = w_keyval.reshape(D // 2, N_TP, 2, KV_PART).transpose(0, 2, 1, 3).reshape(D, 2 * KVH * HD)
    pages_plain = pool_pages.reshape(POOL_PAGES, N_TP, PAGE, KV_PART).transpose(0, 2, 1, 3).reshape(POOL_PAGES, PAGE, 2 * KVH * HD)

    def run_group(inputs):
        return one_group(inputs[0], inputs[1], inputs[2], inputs[3], w_query, keyval_matrix, w_out, pages_plain)
    mixed, outgoing = lax.map(run_group, (tokens.reshape(N_POOL, GROUP, D), lengths, hit_pages, new_owner))
    new_store = outgoing.transpose(1, 0, 2, 3, 4).reshape(N_POOL * N_POOL * CAPN, N_TP, PAGE * KV_PART)
    return (mixed.reshape(TOKENS, D), new_store)
```

```python
import functools
import math

import jax
import jax.numpy as jnp
from jax import lax
from jax.experimental import pallas as pl
from jax.experimental.pallas import tpu as pltpu
from jax.sharding import PartitionSpec as P

KVH = 8
HD = 128
PAGE = 32
REQS = 4
HITS = 4
CAPF = 6
CAPN = 2


EPSILON = 1e-06
ROPE_BASE = 1000000.0


def shortened(value):
    return jax.tree.map(lambda a: a.astype(jnp.bfloat16) if a.dtype == jnp.float32 else a, value)


def partner(value, axis, stride):
    mask = 2**stride
    pairs = [(source, source ^ mask) for source in range(lax.axis_size(axis))]
    return lax.ppermute(value, axis, pairs)


def rotate(values, positions):
    half = values.shape[-1] // 2
    steps_range = jnp.arange(half, dtype=jnp.float32)
    frequency = ROPE_BASE ** (-2.0 * steps_range / values.shape[-1])
    angles = positions.astype(jnp.float32)[:, None, None] * frequency[None, None, :]
    cosine = jnp.cos(angles)
    sine = jnp.sin(angles)
    first_half = values[..., :half]
    second_half = values[..., half:]
    return jnp.concatenate(
        [first_half * cosine - second_half * sine, second_half * cosine + first_half * sine],
        axis=-1,
    )


def slot_table(owners_row, capacity, seats):
    count_items = owners_row.shape[0]
    item_index = jnp.arange(count_items, dtype=jnp.int32)
    earlier_same = (owners_row[:, None] == owners_row[None, :]) & (
        item_index[None, :] < item_index[:, None]
    )
    slots = jnp.sum(earlier_same.astype(jnp.int32), axis=1)
    targets = owners_row * capacity + slots
    seat_index = jnp.arange(seats, dtype=jnp.int32)
    return targets[:, None] == seat_index[None, :]


def join_stack(held_new, held_cached, upper_half, other_new, other_cached):
    held_new = jnp.where(
        upper_half,
        jnp.concatenate([other_new, held_new], axis=0),
        jnp.concatenate([held_new, other_new], axis=0),
    )
    held_cached = jnp.where(
        upper_half,
        jnp.concatenate([other_cached, held_cached], axis=0),
        jnp.concatenate([held_cached, other_cached], axis=0),
    )
    return (held_new, held_cached)


def unstack_columns(held):
    return held.transpose(1, 0, 2).reshape(held.shape[1], held.shape[0] * held.shape[2])


def body(tokens, lengths, hit_pages, new_owner, w_query, w_keyval, w_out, pool_pages):
    rows_dev = tokens.shape[0]
    tp_count = lax.axis_size("tp")
    pool_count = lax.axis_size("pool")
    tp_rank = lax.axis_index("tp")
    group_rows = rows_dev * tp_count
    query_width = w_query.shape[1]
    part_width = w_keyval.shape[1] // 2
    heads_here = query_width // HD
    sharing = tp_count // KVH
    pages_here = pool_pages.shape[0]
    keyval_local = w_keyval.reshape(w_keyval.shape[0] * 2, part_width)
    pages_flat = pool_pages.reshape(pages_here, pool_pages.shape[1] * pool_pages.shape[2])
    tokens_wide = tokens.astype(jnp.float32)
    normed = (
        tokens_wide
        * lax.rsqrt(jnp.mean(tokens_wide * tokens_wide, axis=1, keepdims=True) + EPSILON)
    ).astype(jnp.bfloat16)
    slices = lax.all_to_all(normed, "pool", split_axis=1, concat_axis=0, tiled=True)
    slices = slices.reshape(pool_count, rows_dev, slices.shape[1])
    row_piece = lax.all_gather(slices, "tp", axis=1, tiled=True)
    partial_terms = jnp.concatenate(
        [
            jnp.einsum("prd,dc->prc", row_piece, w_query, preferred_element_type=jnp.float32),
            jnp.einsum("prd,dc->prc", row_piece, keyval_local, preferred_element_type=jnp.float32),
        ],
        axis=2,
    )
    projected = lax.psum_scatter(
        partial_terms.astype(jnp.bfloat16), "pool", scatter_dimension=0, tiled=True
    )[0].astype(jnp.float32)
    lengths_row = lengths[0]
    ends_at = jnp.cumsum(lengths_row)
    starts_at = ends_at - lengths_row
    token_index = jnp.arange(group_rows, dtype=jnp.int32)
    request_ids = jnp.sum((token_index[:, None] >= ends_at[None, :]).astype(jnp.int32), axis=1)
    chosen = request_ids[:, None] == jnp.arange(REQS, dtype=jnp.int32)[None, :]
    start_of = jnp.sum(jnp.where(chosen, starts_at[None, :], 0), axis=1)
    positions = token_index - start_of + HITS * PAGE
    queries = rotate(
        projected[:, :query_width].reshape(group_rows, heads_here, HD), positions
    ).astype(jnp.bfloat16)
    keyval_part = projected[:, query_width:].astype(jnp.bfloat16)
    page_ids = hit_pages.reshape(-1)
    count_hits = page_ids.shape[0]
    placed_hits = slot_table(page_ids // pages_here, CAPF, pool_count * CAPF)
    wanted = jnp.sum(jnp.where(placed_hits, (page_ids % pages_here)[:, None], 0), axis=0)
    wanted = wanted.reshape(pool_count, CAPF)
    asked = lax.all_to_all(wanted, "pool", split_axis=0, concat_axis=0, tiled=True)
    found = jnp.take(pages_flat, asked.reshape(-1), axis=0)
    found = found.reshape(asked.shape[0], asked.shape[1], pages_flat.shape[1])
    returned = lax.all_to_all(found, "pool", split_axis=0, concat_axis=0, tiled=True)
    returned = returned.reshape(pool_count * CAPF, PAGE * part_width)
    cached_part = jnp.dot(
        placed_hits.astype(jnp.bfloat16), returned, preferred_element_type=jnp.float32
    ).astype(jnp.bfloat16)
    cached_part = cached_part.reshape(count_hits * PAGE, part_width)
    bit_count = sharing.bit_length() - 1
    held_new = keyval_part[None]
    held_cached = cached_part[None]
    for bit_number in range(bit_count):
        other_new, other_cached = (
            partner(shortened(held_new), "tp", bit_number).astype(held_new.dtype),
            partner(shortened(held_cached), "tp", bit_number).astype(held_cached.dtype),
        )
        upper_half = tp_rank // 2**bit_number % 2 == 1
        held_new, held_cached = join_stack(
            held_new, held_cached, upper_half, other_new, other_cached
        )
    new_head = unstack_columns(held_new)
    cached_head = unstack_columns(held_cached)
    new_keys = (
        rotate(new_head[:, :HD].astype(jnp.float32).reshape(group_rows, 1, HD), positions)
        .astype(jnp.bfloat16)
        .reshape(group_rows, HD)
    )
    stored_head = jnp.concatenate([new_keys, new_head[:, HD:]], axis=1)
    own_columns = lax.dynamic_slice_in_dim(
        stored_head, tp_rank % sharing * part_width, part_width, 1
    )
    page_count = group_rows // PAGE
    page_rows = own_columns.reshape(page_count, PAGE * part_width)
    placed_new = slot_table(new_owner[0], CAPN, pool_count * CAPN).astype(jnp.bfloat16)
    outgoing = jnp.dot(placed_new.T, page_rows, preferred_element_type=jnp.float32).astype(
        jnp.bfloat16
    )
    outgoing = outgoing.reshape(pool_count, CAPN, PAGE * part_width)
    new_store = lax.all_to_all(outgoing, "pool", split_axis=0, concat_axis=0, tiled=True).reshape(
        pool_count * CAPN, 1, PAGE * part_width
    )
    keys_all = jnp.concatenate([cached_head[:, :HD], new_keys], axis=0)
    values_all = jnp.concatenate([cached_head[:, HD:], new_head[:, HD:]], axis=0)
    cached_rows = count_hits * PAGE
    key_request = jnp.concatenate(
        [jnp.arange(cached_rows, dtype=jnp.int32) // (HITS * PAGE), request_ids]
    )
    key_order = jnp.concatenate([jnp.full((cached_rows,), -1, jnp.int32), token_index])
    block_rows = min(group_rows, 512)

    def attend(first_row):
        scores = jnp.einsum(
            "bhd,kd->hbk", queries, keys_all, preferred_element_type=jnp.float32
        ) / math.sqrt(HD)
        visible = (request_ids[:, None] == key_request[None, :]) & (
            key_order[None, :] <= token_index[:, None]
        )
        scores = jnp.where(visible[None], scores, -jnp.inf)
        highest = jnp.max(scores, axis=-1, keepdims=True)
        expanded = jnp.exp(scores - highest)
        weights = (expanded / jnp.sum(expanded, axis=-1, keepdims=True)).astype(jnp.bfloat16)
        blended = jnp.einsum(
            "hbk,kd->bhd", weights, values_all, preferred_element_type=jnp.float32
        ).astype(jnp.bfloat16)
        return blended.reshape(block_rows, query_width)

    attended = lax.map(
        attend, jnp.arange(group_rows // block_rows, dtype=jnp.int32) * block_rows
    ).reshape(group_rows, query_width)
    every = lax.all_gather(attended, "pool", axis=0, tiled=False)
    parts = jnp.einsum("prd,dc->prc", every, w_out, preferred_element_type=jnp.float32)
    scattered = lax.psum_scatter(
        parts.astype(jnp.bfloat16), "tp", scatter_dimension=1, tiled=True
    )
    summed = lax.all_to_all(scattered, "pool", split_axis=0, concat_axis=2, tiled=True)
    summed = summed.reshape(rows_dev, tokens.shape[1]).astype(jnp.float32)
    mixed = tokens_wide + summed
    return (mixed, new_store)


MESH = pl.DeviceIdType.MESH
VMEM_BYTES = 56 * 1024 * 1024
CORES = 2


def remote(source, target, send_sem, recv_sem, device):
    return pltpu.make_async_remote_copy(
        src_ref=source,
        dst_ref=target,
        send_sem=send_sem,
        recv_sem=recv_sem,
        device_id=device,
        device_id_type=MESH,
    )


def places(pools, chips):
    pool = lax.axis_index("pool")
    rank = lax.axis_index("tp")
    chip, core = rank // CORES, rank % CORES
    pool_peers = [lax.rem(pool + k, pools) for k in range(1, pools)]
    chip_peers = [lax.rem(chip + k, chips) for k in range(1, chips)]
    return pool, rank, chip, core, pool_peers, chip_peers


def meet(pool, rank, chip, core, pool_peers, chip_peers):
    barrier = pltpu.get_barrier_semaphore()
    devices = [(peer, rank) for peer in pool_peers]
    devices += [(pool, peer * CORES + core) for peer in chip_peers]
    devices += [(pool, chip * CORES + 1 - core)]
    for device in devices:
        pl.semaphore_signal(barrier, inc=1, device_id=device, device_id_type=MESH)
    pl.semaphore_wait(barrier, len(devices))


def project_kernel(
    pools, chips, seats,
    tokens_ref, wanted_ref, query_ref, keyval_ref, pages_ref,
    projected_ref, fetched_ref,
    normed, rows, weights, store, ids, numbers, page_out, page_in, part_out, part_in, own,
    load_sem, id_send, id_recv, number_sem, pool_send, row_recv, chip_send, side_send,
    page_send, page_recv, part_send, part_recv,
):
    pool, rank, chip, core, pool_peers, chip_peers = places(pools, chips)
    depth = rows.shape[3]
    query_width = query_ref.shape[1]
    width = weights.shape[1]
    page, part = page_out.shape[2:]
    sibling = (pool, chip * CORES + 1 - core)
    loads = [
        pltpu.make_async_copy(pages_ref, store, load_sem.at[0]),
        pltpu.make_async_copy(query_ref, weights.at[:, pl.ds(0, query_width)], load_sem.at[1]),
        pltpu.make_async_copy(
            keyval_ref, weights.at[:, pl.ds(query_width, width - query_width)], load_sem.at[2]
        ),
    ]
    for load in loads:
        load.start()
    wide = tokens_ref[...].astype(jnp.float32)
    scale = lax.rsqrt(jnp.mean(wide * wide, axis=1, keepdims=True) + EPSILON)
    scaled = (wide * scale).astype(jnp.bfloat16)
    for p in range(pools):
        normed[p] = scaled[:, p * depth : (p + 1) * depth]
    rows[pool, rank] = normed[pool]
    ids[pool] = wanted_ref[pool]
    meet(pool, rank, chip, core, pool_peers, chip_peers)
    sends = []

    def send(copy):
        copy.start()
        sends.append(copy)

    for peer in pool_peers:
        send(remote(wanted_ref.at[peer], ids.at[pool], id_send.at[peer], id_recv.at[pool], (peer, rank)))
    for peer in pool_peers:
        send(
            remote(normed.at[peer], rows.at[pool, rank], pool_send.at[peer], row_recv.at[pool, rank], (peer, rank))
        )

    def arrived(group, source):
        block = rows.at[group, source]
        remote(block, block, side_send.at[group, source], row_recv.at[group, source], sibling).wait_recv()

    def to_sibling(group, source):
        block = rows.at[group, source]
        send(remote(block, block, side_send.at[group, source], row_recv.at[group, source], sibling))

    def to_chips(group):
        block = rows.at[group, rank]
        for peer in chip_peers:
            send(
                remote(
                    block, block, chip_send.at[group, peer], row_recv.at[group, rank], (pool, peer * CORES + core)
                )
            )
        to_sibling(group, rank)

    to_chips(pool)
    for peer in pool_peers:
        arrived(peer, rank)
        to_chips(peer)

    for peer in pool_peers:
        remote(ids.at[peer], ids.at[peer], id_send.at[peer], id_recv.at[peer], (peer, rank)).wait_recv()
    numbers_copy = pltpu.make_async_copy(ids, numbers, number_sem)
    numbers_copy.start()
    numbers_copy.wait()
    loads[0].wait()
    block_rows = store.shape[1]
    lane = lax.broadcasted_iota(jnp.int32, (page, page * block_rows), 1)
    line = lax.broadcasted_iota(jnp.int32, (page, page * block_rows), 0)
    offset = lane - line * block_rows

    def fetch(group):
        def one(seat, carry):
            block = store[numbers[group, 0, seat]]
            tall = jnp.concatenate([block[:, t * part : (t + 1) * part] for t in range(page)], axis=0)
            chosen = (offset == numbers[group, 1, seat]).astype(jnp.float32).astype(jnp.bfloat16)
            page_out[group, seat] = jnp.dot(chosen, tall, preferred_element_type=jnp.float32).astype(jnp.bfloat16)
            return carry

        lax.fori_loop(0, seats, one, 0)

    def pass_on(group):
        for peer in chip_peers:
            arrived(group, peer * CORES + core)
            to_sibling(group, peer * CORES + core)

    def multiply(group):
        for c in range(chips):
            arrived(group, c * CORES + 1 - core)
        left = rows[group].reshape(rows.shape[1] * rows.shape[2], depth)
        return left

    step = 256 if width % 256 == 0 else 128

    def project(group, target, dtype):
        left = multiply(group)

        def one(c, carry):
            columns = pl.ds(pl.multiple_of(c * step, step), step)
            target[:, columns] = jnp.dot(left, weights[:, columns], preferred_element_type=jnp.float32).astype(dtype)
            return carry

        lax.fori_loop(0, width // step, one, 0)

    pass_on(pool)
    for index, peer in enumerate(pool_peers):
        fetch(peer)
        send(remote(page_out.at[peer], page_in.at[pool], page_send.at[peer], page_recv.at[pool], (peer, rank)))
        pass_on(peer)
        if index == 0:
            loads[1].wait()
            loads[2].wait()
        project(peer, part_out.at[peer], jnp.bfloat16)
        send(remote(part_out.at[peer], part_in.at[pool], part_send.at[peer], part_recv.at[pool], (peer, rank)))
    project(pool, own, jnp.float32)
    fetch(pool)
    for peer in pool_peers:
        remote(page_in.at[peer], page_in.at[peer], page_send.at[peer], page_recv.at[peer], (peer, rank)).wait_recv()
    for p in range(pools):
        fetched_ref[p] = page_in[p]
    fetched_ref[pool] = page_out[pool]
    for peer in pool_peers:
        remote(part_in.at[peer], part_in.at[peer], part_send.at[peer], part_recv.at[peer], (peer, rank)).wait_recv()
    total = own[...]
    for peer in pool_peers:
        total = total + part_in[peer].astype(jnp.float32)
    projected_ref[...] = total
    for copy in sends:
        copy.wait_send()


def output_kernel(
    pools, chips, heads, halves, new_seats,
    tokens_ref, projected_ref, fetched_ref, cosine_ref, sine_ref, request_ref, key_request_ref, placed_ref, out_ref,
    mixed_ref, store_ref,
    weights, keys, values, page_out, page_in, attended, parts, side_in, chip_out, chip_in, last_out, last_in,
    load_sem, page_send, page_recv, att_send, att_recv, side_send, side_recv, chip_send, chip_recv,
    last_send, last_recv,
):
    pool, rank, chip, core, pool_peers, chip_peers = places(pools, chips)
    sibling = (pool, chip * CORES + 1 - core)
    load = pltpu.make_async_copy(out_ref, weights, load_sem)
    load.start()
    group_rows = projected_ref.shape[0]
    cached_rows = keys.shape[0] - group_rows
    query_width = heads * HD
    cosine, sine = cosine_ref[...], sine_ref[...]

    def turned(part):
        return part * cosine + pltpu.roll(part, HD // 2, axis=1) * sine

    new_keys = projected_ref[:, query_width : query_width + HD].astype(jnp.bfloat16).astype(jnp.float32)
    new_keys = turned(new_keys).astype(jnp.bfloat16)
    new_values = projected_ref[:, query_width + HD :].astype(jnp.bfloat16)
    cached = fetched_ref[...].reshape(cached_rows, 2 * HD)
    keys[0:cached_rows] = cached[:, :HD]
    values[0:cached_rows] = cached[:, HD:]
    keys[cached_rows:] = new_keys
    values[cached_rows:] = new_values
    count = group_rows // PAGE
    stored = jnp.concatenate([new_keys.astype(jnp.float32), new_values.astype(jnp.float32)], axis=1)
    for seat in range(pools * new_seats):
        total = stored[0:PAGE] * placed_ref[seat]
        for n in range(1, count):
            total = total + stored[n * PAGE : (n + 1) * PAGE] * placed_ref[n * pools * new_seats + seat]
        page_out[seat // new_seats, seat % new_seats] = total.astype(jnp.bfloat16)
    meet(pool, rank, chip, core, pool_peers, chip_peers)
    sends = []

    def send(copy):
        copy.start()
        sends.append(copy)

    row = lax.broadcasted_iota(jnp.int32, (group_rows, keys.shape[0]), 0)
    column = lax.broadcasted_iota(jnp.int32, (group_rows, keys.shape[0]), 1) - cached_rows
    visible = (request_ref[...] == key_request_ref[...]) & (column <= row)
    heads_half = heads // halves
    for half in range(halves):
        for h in range(heads_half):
            first = (half * heads_half + h) * HD
            query = turned(projected_ref[:, first : first + HD]).astype(jnp.bfloat16)
            scores = lax.dot_general(
                query, keys[...], (((1,), (1,)), ((), ())), preferred_element_type=jnp.float32
            ) * (1.0 / math.sqrt(HD))
            scores = jnp.where(visible, scores, -jnp.inf)
            grown = jnp.exp(scores - jnp.max(scores, axis=1, keepdims=True))
            share = (grown * (1.0 / jnp.sum(grown, axis=1, keepdims=True))).astype(jnp.bfloat16)
            attended[pool, half, :, h * HD : (h + 1) * HD] = jnp.dot(
                share, values[...], preferred_element_type=jnp.float32
            ).astype(jnp.bfloat16)
        block = attended.at[pool, half]
        for peer in pool_peers:
            send(remote(block, block, att_send.at[peer, half], att_recv.at[pool, half], (peer, rank)))
    for peer in pool_peers:
        send(remote(page_out.at[peer], page_in.at[pool], page_send.at[peer], page_recv.at[pool], (peer, rank)))
    load.wait()
    half_width = heads_half * HD
    rows_dev, width = parts.shape[3:]
    step = 512 if width % 512 == 0 else 128

    def multiply(group):
        def one(c, carry):
            columns = pl.ds(pl.multiple_of(c * step, step), step)
            total = jnp.dot(attended[group, 0], weights[0:half_width, columns], preferred_element_type=jnp.float32)
            for half in range(1, halves):
                total = total + jnp.dot(
                    attended[group, half],
                    weights[half * half_width : (half + 1) * half_width, columns],
                    preferred_element_type=jnp.float32,
                )
            parts[group, :, :, :, columns] = total.astype(jnp.bfloat16).reshape(chips, CORES, rows_dev, step)
            return carry

        lax.fori_loop(0, width // step, one, 0)
        send(remote(parts.at[group, :, 1 - core], side_in.at[group], side_send.at[group], side_recv.at[group], sibling))

    def join_side(group):
        remote(side_in.at[group], side_in.at[group], side_send.at[group], side_recv.at[group], sibling).wait_recv()
        total = parts[group, :, core].astype(jnp.float32) + side_in[group].astype(jnp.float32)
        chip_out[group] = total.astype(jnp.bfloat16)
        for peer in chip_peers:
            send(
                remote(
                    chip_out.at[group, peer], chip_in.at[group, chip],
                    chip_send.at[group, peer], chip_recv.at[group, chip], (pool, peer * CORES + core),
                )
            )

    def join_chips(group):
        total = chip_out[group, chip].astype(jnp.float32)
        for peer in chip_peers:
            block = chip_in.at[group, peer]
            remote(
                block, block, chip_send.at[group, peer], chip_recv.at[group, peer], (pool, peer * CORES + core)
            ).wait_recv()
            total = total + chip_in[group, peer].astype(jnp.float32)
        return total

    order = [pool] + pool_peers
    for index in range(pools + 2):
        if index < pools:
            group = order[index]
            if index:
                for half in range(halves):
                    block = attended.at[group, half]
                    remote(block, block, att_send.at[group, half], att_recv.at[group, half], (group, rank)).wait_recv()
            multiply(group)
        if 1 <= index <= pools:
            join_side(order[index - 1])
        if index >= 2:
            group = order[index - 2]
            total = join_chips(group)
            last_out[group] = total.astype(jnp.bfloat16)
            if index > 2:
                send(
                    remote(last_out.at[group], last_in.at[pool], last_send.at[group], last_recv.at[pool], (group, rank))
                )
    last_in[pool] = last_out[pool]
    for peer in pool_peers:
        remote(page_in.at[peer], page_in.at[peer], page_send.at[peer], page_recv.at[peer], (peer, rank)).wait_recv()
    page_in[pool] = page_out[pool]
    store_ref[...] = page_in[...].reshape(store_ref.shape)
    for peer in pool_peers:
        remote(last_in.at[peer], last_in.at[peer], last_send.at[peer], last_recv.at[peer], (peer, rank)).wait_recv()
    for p in range(pools):
        columns = slice(p * width, (p + 1) * width)
        mixed_ref[:, columns] = tokens_ref[:, columns].astype(jnp.float32) + last_in[p].astype(jnp.float32)
    for copy in sends:
        copy.wait_send()


def fused(tokens, lengths, hit_pages, new_owner, w_query, w_keyval, w_out, pool_pages):
    rows_dev, features = tokens.shape
    pools, ranks = lax.axis_size("pool"), lax.axis_size("tp")
    chips = ranks // CORES
    group_rows = rows_dev * ranks
    query_width = w_query.shape[1]
    heads = query_width // HD
    part = w_keyval.shape[1] // 2
    width = query_width + part
    depth = w_query.shape[0]
    pages_here = pool_pages.shape[0]
    block_rows = 16
    keyval = w_keyval.reshape(depth, part)
    store = pool_pages.reshape(pages_here // block_rows, block_rows, PAGE * part)

    page_ids = hit_pages.reshape(-1)
    placed_hits = slot_table(page_ids // pages_here, CAPF, pools * CAPF)
    local = (page_ids % pages_here)[:, None]
    wanted = jnp.sum(jnp.where(placed_hits, local, 0), axis=0).reshape(pools, 1, CAPF)
    wanted = jnp.concatenate([wanted // block_rows, wanted % block_rows], axis=1)
    wanted = jnp.pad(wanted, ((0, 0), (0, 6), (0, 128 - CAPF)))
    hit_request = jnp.arange(page_ids.shape[0], dtype=jnp.int32)[:, None] // HITS
    seat_request = jnp.sum(jnp.where(placed_hits, hit_request + 1, 0), axis=0) - 1

    lengths_row = lengths[0]
    ends_at = jnp.cumsum(lengths_row)
    starts_at = ends_at - lengths_row
    token_index = jnp.arange(group_rows, dtype=jnp.int32)
    request_ids = jnp.sum((token_index[:, None] >= ends_at[None, :]).astype(jnp.int32), axis=1)
    chosen = request_ids[:, None] == jnp.arange(REQS, dtype=jnp.int32)[None, :]
    start_of = jnp.sum(jnp.where(chosen, starts_at[None, :], 0), axis=1)
    positions = token_index - start_of + HITS * PAGE
    half = HD // 2
    frequency = ROPE_BASE ** (-2.0 * jnp.arange(half, dtype=jnp.float32) / HD)
    angles = positions.astype(jnp.float32)[:, None] * frequency[None, :]
    cosine, sine = jnp.cos(angles), jnp.sin(angles)
    cosine = jnp.concatenate([cosine, cosine], axis=1)
    sine = jnp.concatenate([-sine, sine], axis=1)
    key_request = jnp.concatenate([jnp.repeat(seat_request, PAGE), request_ids])[None, :]
    placed_new = slot_table(new_owner[0], CAPN, pools * CAPN).astype(jnp.float32).reshape(-1)

    vmem = pl.BlockSpec(memory_space=pltpu.VMEM)
    smem = pl.BlockSpec(memory_space=pltpu.SMEM)
    anywhere = pl.BlockSpec(memory_space=pl.ANY)
    bf16, f32 = jnp.bfloat16, jnp.float32
    dma = pltpu.SemaphoreType.DMA
    projected, fetched = pl.pallas_call(
        functools.partial(project_kernel, pools, chips, CAPF),
        out_shape=(
            jax.ShapeDtypeStruct((group_rows, width), f32),
            jax.ShapeDtypeStruct((pools, CAPF, PAGE, part), bf16),
        ),
        in_specs=[vmem, vmem, anywhere, anywhere, anywhere],
        out_specs=(vmem, vmem),
        scratch_shapes=[
            pltpu.VMEM((pools, rows_dev, depth), bf16),
            pltpu.VMEM((pools, ranks, rows_dev, depth), bf16),
            pltpu.VMEM((depth, width), bf16),
            pltpu.VMEM(store.shape, bf16),
            pltpu.VMEM(wanted.shape, jnp.int32),
            pltpu.SMEM(wanted.shape, jnp.int32),
            pltpu.VMEM((pools, CAPF, PAGE, part), bf16),
            pltpu.VMEM((pools, CAPF, PAGE, part), bf16),
            pltpu.VMEM((pools, group_rows, width), bf16),
            pltpu.VMEM((pools, group_rows, width), bf16),
            pltpu.VMEM((group_rows, width), f32),
            dma((3,)),
            dma((pools,)),
            dma((pools,)),
            dma(()),
            dma((pools,)),
            dma((pools, ranks)),
            dma((pools, chips)),
            dma((pools, ranks)),
            dma((pools,)),
            dma((pools,)),
            dma((pools,)),
            dma((pools,)),
        ],
        compiler_params=pltpu.CompilerParams(
            collective_id=0, has_side_effects=True, vmem_limit_bytes=VMEM_BYTES
        ),
        name="project",
    )(tokens, wanted, w_query, keyval, store)

    halves = 2 if heads % 2 == 0 else 1
    keys_count = pools * CAPF * PAGE + group_rows
    mixed, stored = pl.pallas_call(
        functools.partial(output_kernel, pools, chips, heads, halves, CAPN),
        out_shape=(
            jax.ShapeDtypeStruct((rows_dev, features), f32),
            jax.ShapeDtypeStruct((pools * CAPN, PAGE, part), bf16),
        ),
        in_specs=[vmem] * 7 + [smem, anywhere],
        out_specs=(vmem, vmem),
        scratch_shapes=[
            pltpu.VMEM(w_out.shape, bf16),
            pltpu.VMEM((keys_count, HD), bf16),
            pltpu.VMEM((keys_count, HD), bf16),
            pltpu.VMEM((pools, CAPN, PAGE, part), bf16),
            pltpu.VMEM((pools, CAPN, PAGE, part), bf16),
            pltpu.VMEM((pools, halves, group_rows, query_width // halves), bf16),
            pltpu.VMEM((pools, chips, CORES, rows_dev, w_out.shape[1]), bf16),
            pltpu.VMEM((pools, chips, rows_dev, w_out.shape[1]), bf16),
            pltpu.VMEM((pools, chips, rows_dev, w_out.shape[1]), bf16),
            pltpu.VMEM((pools, chips, rows_dev, w_out.shape[1]), bf16),
            pltpu.VMEM((pools, rows_dev, w_out.shape[1]), bf16),
            pltpu.VMEM((pools, rows_dev, w_out.shape[1]), bf16),
            dma(()),
            dma((pools,)),
            dma((pools,)),
            dma((pools, halves)),
            dma((pools, halves)),
            dma((pools,)),
            dma((pools,)),
            dma((pools, chips)),
            dma((pools, chips)),
            dma((pools,)),
            dma((pools,)),
        ],
        compiler_params=pltpu.CompilerParams(
            collective_id=1, has_side_effects=True, vmem_limit_bytes=VMEM_BYTES
        ),
        name="output",
    )(tokens, projected, fetched, cosine, sine, request_ids[:, None], key_request, placed_new, w_out)
    return (mixed, stored.reshape(pools * CAPN, 1, PAGE * part))


def solution(mesh):
    whole_heads = mesh.shape["tp"] == KVH
    return jax.shard_map(
        fused if whole_heads else body,
        mesh=mesh,
        in_specs=(
            P(("pool", "tp"), None),
            P("pool", None),
            P("pool", None, None),
            P("pool", None),
            P("pool", "tp"),
            P("pool", "tp"),
            P("tp", "pool"),
            P("pool", "tp", None),
        ),
        out_specs=(P(("pool", "tp"), None), P("pool", "tp", None)),
        check_vma=False,
    )
```
